128 devices in a mesh: row: 16 (over y, x_lo, core), col: 8 (over x_hi, z).
Axes of the slice: x: 4 (x_hi: 2, x_lo: 2; x = x_hi * 2 + x_lo), y: 4, z: 4, core: 2. Of those that a mesh axis runs over, the one named last changes fastest.
Arguments:
- inputs: bfloat16 [2048, 6144], P('col', 'row'), may hold values from -6 to 6
- cotangent: bfloat16 [2048, 6144], P('col', 'row'), may hold values from -6 to 6
- preact: bfloat16 [2048, 24576], P('row', 'col'), may hold values from -8 to 8
- up_weight: bfloat16 [6144, 24576], P('row', 'col'), may hold values from -0.078125 to 0.078125
- down_weight: bfloat16 [24576, 6144], P('col', 'row'), may hold values from -0.0390625 to 0.0390625
Outputs:
- input_grad: bfloat16 [2048, 6144], P('col', 'row')
- up_grad: bfloat16 [6144, 24576], P('row', 'col')
- down_grad: bfloat16 [24576, 6144], P('col', 'row')
The draws below stay inside these ranges and needn't reach their ends.
All inputs are finite; a program needn't handle non-finite values.
Results may differ from the reference program's by a relative error of at most 0.03.
Values may be sent and summed in bfloat16 or wider, within the bound.
No kernel may reach another device: no remote copies, remote signals or barrier semaphores. Data moves between devices by JAX's collectives and lax.ppermute only.
A program may use at most 128 MiB of HBM per device.

```python
import math
import jax
import jax.numpy as jnp
from jax import lax

D = 6144
FF = 24576
TOKENS = 2048
N_ROW = 16
N_COL = 8


def levels(own_key, dims, cuts, smallest, high):
    def one(axis_at, parts):
        steps = jax.random.uniform(jax.random.fold_in(jax.random.fold_in(own_key, 6), axis_at), (parts,), jnp.float32, smallest / len(cuts), high / len(cuts))
        return jnp.repeat(jnp.exp(steps), dims[axis_at] // parts).reshape((-1,) + (1,) * (len(dims) - axis_at - 1))

    gain = one(*cuts[0])
    for cut in cuts[1:]:
        gain = gain * one(*cut)
    return gain


def normal_values(key, extent, scale, bound, split=(), held_as=jnp.bfloat16):
    drawn = scale * jax.random.normal(key, extent, jnp.float32)
    if split:
        drawn = drawn * levels(key, extent, split, -0.22, 0.18)
    return jnp.clip(drawn, -bound, bound).astype(held_as)


def setup_inputs(seed: int = 0) -> dict:
    arg_keys = jax.random.split(jax.random.key(seed), 6)
    return {
        "inputs": normal_values(arg_keys[0], (TOKENS, D), 1.0, 6.0, ((0, 8), (1, 16))),
        "cotangent": normal_values(arg_keys[1], (TOKENS, D), 1.0, 6.0, ((0, 8), (1, 16))),
        "preact": normal_values(arg_keys[2], (TOKENS, FF), 1.5, 8.0, ((0, 16), (1, 8))),
        "up_weight": normal_values(arg_keys[3], (D, FF), D ** -0.5, 0.078125, ((0, 16), (1, 8))),
        "down_weight": normal_values(arg_keys[4], (FF, D), FF ** -0.5, 0.0390625, ((0, 8), (1, 16))),
    }


gelu_coeff = 0.7978845608
cubic_coeff = 0.044715

def gelu_parts(preact):
    value = preact.astype(jnp.float32)
    tangent = jnp.tanh(gelu_coeff * (value + cubic_coeff * value * value * value))
    activation = 0.5 * value * (1.0 + tangent)
    slope = 0.5 * (1.0 + tangent) + 0.5 * value * (1.0 - tangent * tangent) * gelu_coeff * (1.0 + 3.0 * cubic_coeff * value * value)
    return (activation, slope)

def reference(inputs, cotangent, preact, up_weight, down_weight):
    feature_block = D // N_ROW
    hidden_block = FF // N_COL

    def add_hidden(index, running):
        offset = (index * feature_block).astype(jnp.int32)
        cot_block = lax.dynamic_slice_in_dim(cotangent, offset, feature_block, 1)
        weight_block = lax.dynamic_slice_in_dim(down_weight, offset, feature_block, 1)
        partial_sum = lax.dot_general(cot_block, weight_block, (((1,), (1,)), ((), ())), preferred_element_type=jnp.float32)
        rounded = lax.optimization_barrier(partial_sum.astype(jnp.bfloat16))
        return running + rounded.astype(jnp.float32)
    hidden_grad = lax.fori_loop(0, N_ROW, add_hidden, jnp.zeros((TOKENS, FF), jnp.float32))
    activation, slope = gelu_parts(preact)
    activation = activation.astype(jnp.bfloat16)
    pre_grad = (hidden_grad * slope).astype(jnp.bfloat16)
    scale = 1.0 / math.sqrt(TOKENS)
    down_grad = (lax.dot_general(activation, cotangent, (((0,), (0,)), ((), ())), preferred_element_type=jnp.float32) * scale).astype(jnp.bfloat16)
    up_grad = (lax.dot_general(inputs, pre_grad, (((0,), (0,)), ((), ())), preferred_element_type=jnp.float32) * scale).astype(jnp.bfloat16)

    def add_input(index, running):
        offset = (index * hidden_block).astype(jnp.int32)
        grad_block = lax.dynamic_slice_in_dim(pre_grad, offset, hidden_block, 1)
        weight_block = lax.dynamic_slice_in_dim(up_weight, offset, hidden_block, 1)
        partial_sum = lax.dot_general(grad_block, weight_block, (((1,), (1,)), ((), ())), preferred_element_type=jnp.float32)
        rounded = lax.optimization_barrier(partial_sum.astype(jnp.bfloat16))
        return running + rounded.astype(jnp.float32)
    input_grad = lax.fori_loop(0, N_COL, add_input, jnp.zeros((TOKENS, D), jnp.float32))
    return (input_grad.astype(jnp.bfloat16), up_grad, down_grad)
```

```python
import math

import jax
import jax.numpy as jnp
from jax import lax
from jax.sharding import PartitionSpec as P

gelu_coeff = 0.7978845608
cubic_coeff = 0.044715


def row_pairs(flip):
    pairs = []
    for y in range(4):
        for x in range(2):
            for core in range(2):
                to_y, to_x, to_core = flip(y, x, core)
                pairs.append(((y * 2 + x) * 2 + core, (to_y * 2 + to_x) * 2 + to_core))
    return ("row", pairs)


def col_pairs(flip):
    pairs = []
    for x in range(2):
        for z in range(4):
            to_x, to_z = flip(x, z)
            pairs.append((x * 4 + z, to_x * 4 + to_z))
    return ("col", pairs)


core_swap = row_pairs(lambda y, x, core: (y, x, 1 - core))
row_cube = (
    row_pairs(lambda y, x, core: (y ^ 1, x, core)),
    row_pairs(lambda y, x, core: (3 - y, x, core)),
    row_pairs(lambda y, x, core: (y, 1 - x, core)),
)
col_cube = (
    col_pairs(lambda x, z: (x, z ^ 1)),
    col_pairs(lambda x, z: (x, 3 - z)),
    col_pairs(lambda x, z: (1 - x, z)),
)


def send(block, pairing):
    return lax.ppermute(block, pairing[0], pairing[1])


def ring_bits(place):
    high = place // 2
    return (high ^ (place % 2), high)


def ring_place(low, high):
    return high * 2 + (low ^ high)


def gelu_parts(preact):
    value = preact.astype(jnp.float32)
    tangent = jnp.tanh(gelu_coeff * (value + cubic_coeff * value * value * value))
    activation = 0.5 * value * (1.0 + tangent)
    slope = 0.5 * (1.0 + tangent) + 0.5 * value * (1.0 - tangent * tangent) * gelu_coeff * (
        1.0 + 3.0 * cubic_coeff * value * value
    )
    return (activation, slope)


def contract_last(left, right):
    return lax.dot_general(
        left, right, (((1,), (1,)), ((), ())), preferred_element_type=jnp.float32
    )


def contract_first(left, right):
    return lax.dot_general(
        left, right, (((0,), (0,)), ((), ())), preferred_element_type=jnp.float32
    )


def thirds(block):
    width = block.shape[1] // 3
    return [block[:, part * width : (part + 1) * width] for part in range(3)]


def cube_gather(parts, cube):
    held = [part[None, None, None] for part in parts]
    for step in range(3):
        got = [send(held[s], cube[(s + step) % 3]) for s in range(3)]
        held = [jnp.concatenate([held[s], got[s]], axis=(s + step) % 3) for s in range(3)]
    return held


def cube_scatter(own, away, cube):
    total = own
    for step in (2, 1, 0):
        got = [send(away[s], cube[(s + step) % 3]) for s in range(3)]
        total = [total[s].astype(jnp.float32) + got[s].astype(jnp.float32) for s in range(3)]
        if step:
            axes = [(s + step - 1) % 3 for s in range(3)]
            total = [total[s].astype(jnp.bfloat16) for s in range(3)]
            away = [lax.slice_in_dim(total[s], 1, 2, axis=axes[s]) for s in range(3)]
            total = [lax.slice_in_dim(total[s], 0, 1, axis=axes[s]) for s in range(3)]
    return total


def by_core(core, own, other, axis):
    return jnp.where(
        core == 0,
        jnp.concatenate([own, other], axis=axis),
        jnp.concatenate([other, own], axis=axis),
    )


def body(inputs, cotangent, preact, up_weight, down_weight):
    row, col = lax.axis_index("row"), lax.axis_index("col")
    core, x_lo, y = row % 2, row // 2 % 2, row // 4
    x_hi, z = col // 4, col % 4
    y_bits, z_bits = ring_bits(y), ring_bits(z)
    half = preact.shape[1] // 2
    rows = inputs.shape[0]
    token_count = rows * 8
    scale = 1.0 / math.sqrt(token_count)

    col_at_row, row_at_col = [], []
    for flips in range(8):
        a, b, c = flips // 4, flips // 2 % 2, flips % 2
        block = ring_place(y_bits[0] ^ a, y_bits[1] ^ b) * 2 + (x_lo ^ c)
        bits = ring_bits(block % 4)
        col_at_row.append((bits[0] ^ z_bits[0]) * 4 + (bits[1] ^ z_bits[1]) * 2 + (block // 4 ^ x_hi))
        block = (x_hi ^ c) * 4 + ring_place(z_bits[0] ^ a, z_bits[1] ^ b)
        bits = ring_bits(block // 2)
        row_at_col.append((bits[0] ^ y_bits[0]) * 4 + (bits[1] ^ y_bits[1]) * 2 + (block % 2 ^ x_lo))

    def pair_features(block):
        return jnp.concatenate([block, send(block, core_swap)], axis=1)

    def gather_tokens(block):
        parts = cube_gather(thirds(pair_features(block)), col_cube)
        whole = jnp.concatenate(parts, axis=4).reshape(8, rows, -1)
        picked = [lax.dynamic_index_in_dim(whole, at, 0, keepdims=False) for at in col_at_row]
        return jnp.stack(picked).reshape(2, 2, 2, rows, -1)

    all_cot = gather_tokens(cotangent)

    def own_half(block, axis):
        mine = lax.dynamic_slice_in_dim(block, core * half, half, axis)
        other = lax.dynamic_slice_in_dim(block, (1 - core) * half, half, axis)
        return mine, send(other, core_swap)

    down_half = jnp.concatenate(own_half(down_weight, 0), axis=1)
    mine, other = own_half(preact, 1)
    own_preact = by_core(core, mine, other, 0)
    activation, slope = gelu_parts(own_preact)
    all_act = cube_gather(thirds(activation.astype(jnp.bfloat16)), row_cube)

    third = half // 3
    own, away = [], []
    for s in range(3):
        axis = (s + 2) % 3
        weight = down_half[s * third : (s + 1) * third]
        for at, halves in ((1, away), (0, own)):
            tokens = lax.slice_in_dim(all_cot, at, at + 1, axis=axis)
            product = contract_last(tokens.reshape(4 * rows, -1), weight).astype(jnp.bfloat16)
            halves.append(product.reshape(tokens.shape[:4] + (third,)))
    hidden = cube_scatter(own, away, row_cube)
    own_pre = [
        (part.reshape(rows, third) * slope[:, s * third : (s + 1) * third]).astype(jnp.bfloat16)
        for s, part in enumerate(hidden)
    ]
    all_pre = cube_gather(own_pre, row_cube)
    all_pre = [part.reshape(token_count, third) for part in all_pre]

    all_inputs = gather_tokens(inputs).reshape(token_count, -1)
    up_half = jnp.concatenate(own_half(up_weight, 1), axis=0)

    cot_rows = all_cot.reshape(token_count, -1)
    down = [
        (contract_first(part.reshape(token_count, third), cot_rows) * scale).astype(jnp.bfloat16)
        for part in all_act
    ]
    down = jnp.concatenate(down, axis=0)
    features = inputs.shape[1]
    down_grad = by_core(core, down[:, :features], send(down[:, features:], core_swap), 0)

    partial = contract_last(jnp.concatenate(all_pre, axis=1), up_half).astype(jnp.bfloat16)
    got = send(partial[:, features:], core_swap)
    partial = (partial[:, :features].astype(jnp.float32) + got.astype(jnp.float32)).astype(jnp.bfloat16)
    blocks = partial.reshape(8, rows, features)
    picked = [lax.dynamic_index_in_dim(blocks, at, 0, keepdims=False) for at in row_at_col]
    picked = jnp.stack(picked).reshape(2, 2, 2, rows, features)
    own, away = [], []
    for s in range(3):
        part = picked[..., s * features // 3 : (s + 1) * features // 3]
        own.append(lax.slice_in_dim(part, 0, 1, axis=(s + 2) % 3))
        away.append(lax.slice_in_dim(part, 1, 2, axis=(s + 2) % 3))
    total = cube_scatter(own, away, col_cube)
    input_grad = jnp.concatenate([part.reshape(rows, -1) for part in total], axis=1).astype(jnp.bfloat16)

    up = [(contract_first(all_inputs, part) * scale).astype(jnp.bfloat16) for part in all_pre]
    up = jnp.concatenate(up, axis=1)
    up_grad = by_core(core, up[:features], send(up[features:], core_swap), 1)
    return (input_grad, up_grad, down_grad)


def solution(mesh):
    return jax.shard_map(
        body,
        mesh=mesh,
        in_specs=(
            P("col", "row"),
            P("col", "row"),
            P("row", "col"),
            P("row", "col"),
            P("col", "row"),
        ),
        out_specs=(P("col", "row"), P("row", "col"), P("col", "row")),
        check_vma=False,
    )
```

```python
import math

import jax
import jax.numpy as jnp
from jax import lax
from jax.experimental.layout import Layout, with_layout_constraint
from jax.sharding import PartitionSpec as P

gelu_coeff = 0.7978845608
cubic_coeff = 0.044715


def row_pairs(flip):
    pairs = []
    for y in range(4):
        for x in range(2):
            for core in range(2):
                to_y, to_x, to_core = flip(y, x, core)
                pairs.append(((y * 2 + x) * 2 + core, (to_y * 2 + to_x) * 2 + to_core))
    return ("row", pairs)


def col_pairs(flip):
    pairs = []
    for x in range(2):
        for z in range(4):
            to_x, to_z = flip(x, z)
            pairs.append((x * 4 + z, to_x * 4 + to_z))
    return ("col", pairs)


core_swap = row_pairs(lambda y, x, core: (y, x, 1 - core))
row_cube = (
    row_pairs(lambda y, x, core: (y ^ 1, x, core)),
    row_pairs(lambda y, x, core: (3 - y, x, core)),
    row_pairs(lambda y, x, core: (y, 1 - x, core)),
)
col_cube = (
    col_pairs(lambda x, z: (x, z ^ 1)),
    col_pairs(lambda x, z: (x, 3 - z)),
    col_pairs(lambda x, z: (1 - x, z)),
)


def row_major(block):
    return with_layout_constraint(block, Layout(major_to_minor=tuple(range(block.ndim))))


def send(block, pairing):
    return row_major(lax.ppermute(row_major(block), pairing[0], pairing[1]))


def ring_bits(place):
    high = place // 2
    return (high ^ (place % 2), high)


def ring_place(low, high):
    return high * 2 + (low ^ high)


def gelu_parts(preact):
    value = preact.astype(jnp.float32)
    tangent = jnp.tanh(gelu_coeff * (value + cubic_coeff * value * value * value))
    activation = 0.5 * value * (1.0 + tangent)
    slope = 0.5 * (1.0 + tangent) + 0.5 * value * (1.0 - tangent * tangent) * gelu_coeff * (
        1.0 + 3.0 * cubic_coeff * value * value
    )
    return (activation, slope)


def contract_last(left, right):
    return lax.dot_general(
        left, right, (((1,), (1,)), ((), ())), preferred_element_type=jnp.float32
    )


def contract_first(left, right):
    return lax.dot_general(
        left, right, (((0,), (0,)), ((), ())), preferred_element_type=jnp.float32
    )


def thirds(block):
    width = block.shape[1] // 3
    return [block[:, part * width : (part + 1) * width] for part in range(3)]


def col_halves(block, crossed):
    both = jnp.stack([block, crossed])[None, None]
    rows = block.shape[0] // 2
    return [both[..., :rows, :], both[..., rows:, :]]


def col_gather_step(held, step):
    got = after_all([send(held[s], col_cube[(s + step) % 2]) for s in range(2)])
    return [jnp.concatenate([held[s], got[s]], axis=(s + step) % 2) for s in range(2)]


def add(left, right):
    return left.astype(jnp.float32) + right.astype(jnp.float32)


def cube_gather_step(held, cube, step):
    got = [send(held[s], cube[(s + step) % 3]) for s in range(3)]
    return [jnp.concatenate([held[s], got[s]], axis=(s + step) % 3) for s in range(3)]


def cube_scatter_step(own, got, cube, step):
    axes = [(s + step) % 3 for s in range(3)]
    total = [add(own[s], got[s]).astype(jnp.bfloat16) for s in range(3)]
    away = [lax.slice_in_dim(total[s], 1, 2, axis=axes[s]) for s in range(3)]
    own = [lax.slice_in_dim(total[s], 0, 1, axis=axes[s]) for s in range(3)]
    return own, [send(away[s], cube[axes[s]]) for s in range(3)]


def after_all(blocks, *earlier):
    return list(lax.optimization_barrier(tuple(blocks) + earlier)[: len(blocks)])


def after(block, *earlier):
    return lax.optimization_barrier((block,) + earlier)[0]


def by_core(core, own, other, axis):
    return jnp.where(
        core == 0,
        jnp.concatenate([own, other], axis=axis),
        jnp.concatenate([other, own], axis=axis),
    )


def body(inputs, cotangent, preact, up_weight, down_weight):
    row, col = lax.axis_index("row"), lax.axis_index("col")
    core, x_lo, y = row % 2, row // 2 % 2, row // 4
    x_hi, z = col // 4, col % 4
    y_bits, z_bits = ring_bits(y), ring_bits(z)
    half = preact.shape[1] // 2
    third = half // 3
    rows, features = inputs.shape
    token_count = rows * 8
    scale = 1.0 / math.sqrt(token_count)

    col_at_row, row_at_col = [], []
    for flips in range(8):
        a, b, c = flips // 4, flips // 2 % 2, flips % 2
        block = ring_place(y_bits[0] ^ a, y_bits[1] ^ b) * 2 + (x_lo ^ c)
        bits = ring_bits(block % 4)
        col_at_row.append((bits[0] ^ z_bits[0]) * 4 + (bits[1] ^ z_bits[1]) * 2 + (block // 4 ^ x_hi))
        block = (x_hi ^ c) * 4 + ring_place(z_bits[0] ^ a, z_bits[1] ^ b)
        bits = ring_bits(block // 2)
        row_at_col.append((bits[0] ^ y_bits[0]) * 4 + (bits[1] ^ y_bits[1]) * 2 + (block % 2 ^ x_lo))

    def halves_of(block, axis):
        mine = lax.dynamic_slice_in_dim(block, core * half, half, axis)
        other = lax.dynamic_slice_in_dim(block, (1 - core) * half, half, axis)
        return mine, other

    def as_parts(block):
        return [part[None, None, None] for part in thirds(block)]

    def in_row_order(blocks, places):
        count = blocks.shape[1]
        picked = [lax.dynamic_index_in_dim(blocks, at, 0, keepdims=False) for at in places]
        ordered = jnp.stack(picked)
        return jnp.concatenate([ordered, send(ordered, core_swap)], axis=2).reshape(2, 2, 2, count, -1)

    mine, other = halves_of(preact, 1)
    other = send(other, core_swap)
    crossed = send(cotangent, col_cube[2])
    activation, slope = gelu_parts(by_core(core, mine, other, 0))
    acts = as_parts(activation.astype(jnp.bfloat16))
    cots = col_halves(cotangent, after(crossed, *acts))
    cots = col_gather_step(cots, 0)
    acts = cube_gather_step(acts, row_cube, 0)
    mine, other = halves_of(down_weight, 0)
    down_half = jnp.concatenate([mine, send(other, core_swap)], axis=1)
    merged = after_all(cots + acts, down_half)
    cots, acts = merged[:2], merged[2:]
    cots = col_gather_step(cots, 1)
    acts = cube_gather_step(acts, row_cube, 1)
    cots = after_all(cots, *acts)
    whole = jnp.concatenate(cots, axis=3).reshape(8, rows, features)
    all_cot = in_row_order(whole, col_at_row)

    def hidden_product(s, at):
        tokens = lax.slice_in_dim(all_cot, at, at + 1, axis=(s + 2) % 3)
        weight = down_half[s * third : (s + 1) * third]
        product = contract_last(tokens.reshape(4 * rows, -1), weight).astype(jnp.bfloat16)
        return row_major(product.reshape(tokens.shape[:4] + (third,)))

    away = [hidden_product(s, 1) for s in range(3)]
    got = [send(away[s], row_cube[(s + 2) % 3]) for s in range(3)]
    own = [hidden_product(s, 0) for s in range(3)]

    own, got = cube_scatter_step(own, got, row_cube, 1)
    own, got = cube_scatter_step(own, got, row_cube, 0)
    crossed = send(after(inputs, *own), col_cube[2])
    got = after_all(got, crossed)
    hidden = [add(own[s], got[s]).reshape(rows, third) for s in range(3)]
    own_pre = [
        (part * slope[:, s * third : (s + 1) * third]).astype(jnp.bfloat16) for s, part in enumerate(hidden)
    ]
    pres = [row_major(part[None, None, None]) for part in own_pre]
    pres = cube_gather_step(pres, row_cube, 0)
    near = col_gather_step(after_all(col_halves(inputs, crossed), *pres), 0)
    pres = cube_gather_step(pres, row_cube, 1)
    pres = after_all(pres, *near)

    halves = [slice(h * rows // 2, (h + 1) * rows // 2) for h in range(2)]
    pres = [[pres[s][..., part, :] for s in range(3)] for part in halves]
    last = [[send(pres[h][s], row_cube[(s + 2) % 3]) for s in range(3)] for h in range(2)]
    near = col_gather_step(after_all(near, *pres[0]), 1)
    mine, other = halves_of(after(up_weight, *pres[0]), 1)
    up_half = jnp.concatenate([mine, send(other, core_swap)], axis=0)
    last[0] = after_all(last[0], up_half, *near)

    own, away, got, all_pre = [], [], [], []
    for h in range(2):
        pre = [jnp.concatenate([pres[h][s], last[h][s]], axis=(s + 2) % 3) for s in range(3)]
        pre = jnp.concatenate([block.reshape(token_count // 2, third) for block in pre], axis=1)
        all_pre.append(pre)
        partial = contract_last(pre, up_half).astype(jnp.bfloat16)
        swapped = send(partial[:, features:], core_swap)
        if h == 0:
            last[1] = after_all(last[1], partial)
        else:
            acts = after_all(acts, *last[1])
            got_acts = [send(acts[s], row_cube[(s + 2) % 3]) for s in range(3)]
        blocks = add(partial[:, :features], swapped).astype(jnp.bfloat16).reshape(8, rows // 2, features)
        picked = [lax.dynamic_index_in_dim(blocks, at, 0, keepdims=False) for at in row_at_col]
        picked = jnp.stack(picked).reshape(2, 2, 2, rows // 2, features)
        own.append(lax.slice_in_dim(picked, 0, 1, axis=h))
        away.append(lax.slice_in_dim(picked, 1, 2, axis=h))
        got.append(send(away[h], col_cube[h]))

    up = 0.0
    for h in range(2):
        given = after(near[h], *away).reshape(8, rows // 2, features)
        given = in_row_order(given, col_at_row).reshape(token_count // 2, -1)
        up = up + contract_first(given, all_pre[h])
    up = (up * scale).astype(jnp.bfloat16)

    def down_product(s, *earlier):
        tokens, near_act, far_act = after_all([all_cot, acts[s], got_acts[s]], *earlier)
        act = jnp.concatenate([near_act, far_act], axis=(s + 2) % 3).reshape(token_count, third)
        return (contract_first(act, tokens.reshape(token_count, -1)) * scale).astype(jnp.bfloat16)

    got = after_all(got, up, *got_acts)
    total = [add(own[s], got[s]).astype(jnp.bfloat16) for s in range(2)]
    own = [lax.slice_in_dim(total[s], 0, 1, axis=1 - s) for s in range(2)]
    away = [lax.slice_in_dim(total[s], 1, 2, axis=1 - s) for s in range(2)]
    got = [send(away[s], col_cube[1 - s]) for s in range(2)]
    down = [down_product(s, *away) for s in range(2)]
    got = after_all(got, *down)
    total = [add(own[s], got[s]).astype(jnp.bfloat16)[0, 0] for s in range(2)]
    total = jnp.concatenate(total, axis=1)
    got = send(total[1], col_cube[2])

    down.append(down_product(2, total))
    up = after(up, total)
    up_grad = by_core(core, up[:features], send(up[features:], core_swap), 1)
    down = jnp.concatenate(down, axis=0)
    input_grad = add(total[0], after(got, down)).astype(jnp.bfloat16)
    down_grad = by_core(core, down[:, :features], send(down[:, features:], core_swap), 0)
    return (input_grad, up_grad, down_grad)


def solution(mesh):
    return jax.shard_map(
        body,
        mesh=mesh,
        in_specs=(
            P("col", "row"),
            P("col", "row"),
            P("row", "col"),
            P("row", "col"),
            P("col", "row"),
        ),
        out_specs=(P("col", "row"), P("row", "col"), P("col", "row")),
        check_vma=False,
    )
```

```python
import math

import jax
import jax.numpy as jnp
from jax import lax
from jax.experimental.layout import Layout, with_layout_constraint
from jax.sharding import PartitionSpec as P

gelu_coeff = 0.7978845608
cubic_coeff = 0.044715


def row_pairs(flip):
    pairs = []
    for y in range(4):
        for x in range(2):
            for core in range(2):
                to_y, to_x, to_core = flip(y, x, core)
                pairs.append(((y * 2 + x) * 2 + core, (to_y * 2 + to_x) * 2 + to_core))
    return ("row", pairs)


def col_pairs(flip):
    pairs = []
    for x in range(2):
        for z in range(4):
            to_x, to_z = flip(x, z)
            pairs.append((x * 4 + z, to_x * 4 + to_z))
    return ("col", pairs)


core_swap = row_pairs(lambda y, x, core: (y, x, 1 - core))
row_cube = (
    row_pairs(lambda y, x, core: (y ^ 1, x, core)),
    row_pairs(lambda y, x, core: (3 - y, x, core)),
    row_pairs(lambda y, x, core: (y, 1 - x, core)),
)
col_cube = (
    col_pairs(lambda x, z: (x, z ^ 1)),
    col_pairs(lambda x, z: (x, 3 - z)),
    col_pairs(lambda x, z: (1 - x, z)),
)


def row_major(block):
    return with_layout_constraint(block, Layout(major_to_minor=tuple(range(block.ndim))))


def send(block, pairing):
    return row_major(lax.ppermute(row_major(block), pairing[0], pairing[1]))


def ring_bits(place):
    high = place // 2
    return (high ^ (place % 2), high)


def ring_place(low, high):
    return high * 2 + (low ^ high)


def gelu_parts(preact):
    value = preact.astype(jnp.float32)
    tangent = jnp.tanh(gelu_coeff * (value + cubic_coeff * value * value * value))
    activation = 0.5 * value * (1.0 + tangent)
    slope = 0.5 * (1.0 + tangent) + 0.5 * value * (1.0 - tangent * tangent) * gelu_coeff * (
        1.0 + 3.0 * cubic_coeff * value * value
    )
    return (activation, slope)


def contract_last(left, right):
    return lax.dot_general(
        left, right, (((1,), (1,)), ((), ())), preferred_element_type=jnp.float32
    )


def contract_first(left, right):
    return lax.dot_general(
        left, right, (((0,), (0,)), ((), ())), preferred_element_type=jnp.float32
    )


def thirds(block):
    width = block.shape[1] // 3
    return [block[:, part * width : (part + 1) * width] for part in range(3)]


def col_halves(block, crossed):
    both = jnp.stack([block, crossed])[None, None]
    rows = block.shape[0] // 2
    return [both[..., :rows, :], both[..., rows:, :]]


def col_gather_step(held, step):
    got = after_all([send(held[s], col_cube[(s + step) % 2]) for s in range(2)])
    return [jnp.concatenate([held[s], got[s]], axis=(s + step) % 2) for s in range(2)]


def add(left, right):
    return left.astype(jnp.float32) + right.astype(jnp.float32)


def cube_gather_step(held, cube, step):
    got = [send(held[s], cube[(s + step) % 3]) for s in range(3)]
    return [jnp.concatenate([held[s], got[s]], axis=(s + step) % 3) for s in range(3)]


def cube_scatter_step(own, got, cube, step):
    axes = [(s + step) % 3 for s in range(3)]
    total = [add(own[s], got[s]).astype(jnp.bfloat16) for s in range(3)]
    away = [lax.slice_in_dim(total[s], 1, 2, axis=axes[s]) for s in range(3)]
    own = [lax.slice_in_dim(total[s], 0, 1, axis=axes[s]) for s in range(3)]
    return own, [send(away[s], cube[axes[s]]) for s in range(3)]


def after_all(blocks, *earlier):
    return list(lax.optimization_barrier(tuple(blocks) + earlier)[: len(blocks)])


def after(block, *earlier):
    return lax.optimization_barrier((block,) + earlier)[0]


def by_core(core, own, other, axis):
    return jnp.where(
        core == 0,
        jnp.concatenate([own, other], axis=axis),
        jnp.concatenate([other, own], axis=axis),
    )


def body(inputs, cotangent, preact, up_weight, down_weight):
    row, col = lax.axis_index("row"), lax.axis_index("col")
    core, x_lo, y = row % 2, row // 2 % 2, row // 4
    x_hi, z = col // 4, col % 4
    y_bits, z_bits = ring_bits(y), ring_bits(z)
    half = preact.shape[1] // 2
    third = half // 3
    rows, features = inputs.shape
    token_count = rows * 8
    scale = 1.0 / math.sqrt(token_count)

    col_at_row, row_at_col = [], []
    for flips in range(8):
        a, b, c = flips // 4, flips // 2 % 2, flips % 2
        block = ring_place(y_bits[0] ^ a, y_bits[1] ^ b) * 2 + (x_lo ^ c)
        bits = ring_bits(block % 4)
        col_at_row.append((bits[0] ^ z_bits[0]) * 4 + (bits[1] ^ z_bits[1]) * 2 + (block // 4 ^ x_hi))
        block = (x_hi ^ c) * 4 + ring_place(z_bits[0] ^ a, z_bits[1] ^ b)
        bits = ring_bits(block // 2)
        row_at_col.append((bits[0] ^ y_bits[0]) * 4 + (bits[1] ^ y_bits[1]) * 2 + (block % 2 ^ x_lo))

    def halves_of(block, axis):
        mine = lax.dynamic_slice_in_dim(block, core * half, half, axis)
        other = lax.dynamic_slice_in_dim(block, (1 - core) * half, half, axis)
        return mine, other

    def as_parts(block):
        return [part[None, None, None] for part in thirds(block)]

    def in_row_order(blocks, places):
        count = blocks.shape[1]
        picked = [lax.dynamic_index_in_dim(blocks, at, 0, keepdims=False) for at in places]
        ordered = jnp.stack(picked)
        return jnp.concatenate([ordered, send(ordered, core_swap)], axis=2).reshape(2, 2, 2, count, -1)

    mine, other = halves_of(preact, 1)
    other = send(other, core_swap)
    crossed = send(cotangent, col_cube[2])
    saved = as_parts(by_core(core, mine, other, 0))
    merged = after_all([crossed] + saved)
    crossed, saved = merged[0], merged[1:]
    saved = cube_gather_step(saved, row_cube, 0)
    cots = col_halves(cotangent, crossed)
    cots = col_gather_step(cots, 0)
    acts, slopes = [], []
    for part in saved:
        activation, slope = gelu_parts(part)
        acts.append(activation.astype(jnp.bfloat16))
        slopes.append(slope)
    mine, other = halves_of(down_weight, 0)
    down_half = jnp.concatenate([mine, send(other, core_swap)], axis=1)
    merged = after_all(cots + acts, down_half)
    cots, acts = merged[:2], merged[2:]
    cots = col_gather_step(cots, 1)
    acts = cube_gather_step(acts, row_cube, 1)
    cots = after_all(cots, *acts)
    whole = jnp.concatenate(cots, axis=3).reshape(8, rows, features)
    all_cot = in_row_order(whole, col_at_row)

    def hidden_product(s, at):
        tokens = lax.slice_in_dim(all_cot, at, at + 1, axis=(s + 2) % 3)
        weight = down_half[s * third : (s + 1) * third]
        product = contract_last(tokens.reshape(4 * rows, -1), weight).astype(jnp.bfloat16)
        return row_major(product.reshape(tokens.shape[:4] + (third,)))

    away = [hidden_product(s, 1) for s in range(3)]
    got = [send(away[s], row_cube[(s + 2) % 3]) for s in range(3)]
    own = [hidden_product(s, 0) for s in range(3)]

    own, got = cube_scatter_step(own, got, row_cube, 1)
    crossed = send(after(inputs, *own), col_cube[2])
    got = after_all(got, crossed)
    total = [add(own[s], got[s]).astype(jnp.bfloat16) for s in range(3)]
    got = [send(total[s], row_cube[s]) for s in range(3)]
    pres = []
    for s in range(3):
        near_got, far_got = [lax.slice_in_dim(got[s], at, at + 1, axis=s) for at in (0, 1)]
        hidden = add(total[s], jnp.concatenate([far_got, near_got], axis=s))
        pres.append(row_major((hidden * slopes[s]).astype(jnp.bfloat16)))
    near = col_gather_step(after_all(col_halves(inputs, crossed), *pres), 0)
    pres = cube_gather_step(pres, row_cube, 1)
    pres = after_all(pres, *near)

    last = [send(pres[s], row_cube[(s + 2) % 3]) for s in range(3)]

    near = col_gather_step(after_all(near, *pres), 1)
    mine, other = halves_of(after(up_weight, *pres), 1)
    up_half = jnp.concatenate([mine, send(other, core_swap)], axis=0)
    given = []
    for h in range(2):
        block = near[h].reshape(8, rows // 2, features)
        given.append(in_row_order(block, col_at_row).reshape(token_count // 2, -1))
    last = after_all(last, up_half, *given)

    halves = [slice(h * rows // 2, (h + 1) * rows // 2) for h in range(2)]
    moving = after_all(acts, *last)
    moving = [[act[..., part, :] for act in moving] for part in halves]
    got_acts = [[send(moving[0][s], row_cube[(s + 2) % 3]) for s in range(3)]]
    own, away, got, all_pre = [], [], [], []
    for h, part in enumerate(halves):
        pre = [
            jnp.concatenate([pres[s][..., part, :], last[s][..., part, :]], axis=(s + 2) % 3) for s in range(3)
        ]
        pre = jnp.concatenate([block.reshape(token_count // 2, third) for block in pre], axis=1)
        all_pre.append(pre)
        partial = contract_last(pre, up_half).astype(jnp.bfloat16)
        swapped = send(partial[:, features:], core_swap)
        blocks = add(partial[:, :features], swapped).astype(jnp.bfloat16).reshape(8, rows // 2, features)
        picked = [lax.dynamic_index_in_dim(blocks, at, 0, keepdims=False) for at in row_at_col]
        picked = jnp.stack(picked).reshape(2, 2, 2, rows // 2, features)
        own.append(lax.slice_in_dim(picked, 0, 1, axis=h))
        away.append(lax.slice_in_dim(picked, 1, 2, axis=h))
        if h:
            merged = after_all([away[h]] + moving[1] + got_acts[0])
            away[h], moving[1], got_acts[0] = merged[0], merged[1:4], merged[4:]
            got_acts.append([send(moving[1][s], row_cube[(s + 2) % 3]) for s in range(3)])
        got.append(send(away[h], col_cube[h]))

    up = sum(contract_first(after(given[h], *away), all_pre[h]) for h in range(2))
    up = (up * scale).astype(jnp.bfloat16)

    def down_product(s, *earlier):
        tokens, near_act, first, second = after_all(
            [all_cot, acts[s], got_acts[0][s], got_acts[1][s]], *earlier
        )
        far_act = jnp.concatenate([first, second], axis=3)
        act = jnp.concatenate([near_act, far_act], axis=(s + 2) % 3).reshape(token_count, third)
        return (contract_first(act, tokens.reshape(token_count, -1)) * scale).astype(jnp.bfloat16)

    got = after_all(got, up, *got_acts[1])
    total = [add(own[s], got[s]).astype(jnp.bfloat16) for s in range(2)]
    own = [lax.slice_in_dim(total[s], 0, 1, axis=1 - s) for s in range(2)]
    away = [lax.slice_in_dim(total[s], 1, 2, axis=1 - s) for s in range(2)]
    got = [send(away[s], col_cube[1 - s]) for s in range(2)]
    down = [down_product(s, *away) for s in range(3)]
    got = after_all(got, *down)
    total = [add(own[s], got[s]).astype(jnp.bfloat16)[0, 0] for s in range(2)]
    total = jnp.concatenate(total, axis=1)
    got = send(total[1], col_cube[2])

    down = after_all(down, total)
    up = after(up, total)
    up_grad = by_core(core, up[:features], send(up[features:], core_swap), 1)
    down = jnp.concatenate(down, axis=0)
    down_grad = by_core(core, down[:, :features], send(down[:, features:], core_swap), 0)
    got, up_grad, down_grad = after_all([got, up_grad, down_grad])
    input_grad = add(total[0], got).astype(jnp.bfloat16)
    return (input_grad, up_grad, down_grad)


def solution(mesh):
    return jax.shard_map(
        body,
        mesh=mesh,
        in_specs=(
            P("col", "row"),
            P("col", "row"),
            P("row", "col"),
            P("row", "col"),
            P("col", "row"),
        ),
        out_specs=(P("col", "row"), P("row", "col"), P("col", "row")),
        check_vma=False,
    )
```

```python
import math

import jax
import jax.numpy as jnp
from jax import lax
from jax.experimental.layout import Layout, with_layout_constraint
from jax.sharding import PartitionSpec as P

gelu_coeff = 0.7978845608
cubic_coeff = 0.044715


def row_pairs(flip):
    pairs = []
    for y in range(4):
        for x in range(2):
            for core in range(2):
                to_y, to_x, to_core = flip(y, x, core)
                pairs.append(((y * 2 + x) * 2 + core, (to_y * 2 + to_x) * 2 + to_core))
    return ("row", pairs)


def col_pairs(flip):
    pairs = []
    for x in range(2):
        for z in range(4):
            to_x, to_z = flip(x, z)
            pairs.append((x * 4 + z, to_x * 4 + to_z))
    return ("col", pairs)


core_swap = row_pairs(lambda y, x, core: (y, x, 1 - core))
row_cube = (
    row_pairs(lambda y, x, core: (y ^ 1, x, core)),
    row_pairs(lambda y, x, core: (3 - y, x, core)),
    row_pairs(lambda y, x, core: (y, 1 - x, core)),
)
col_cube = (
    col_pairs(lambda x, z: (x, z ^ 1)),
    col_pairs(lambda x, z: (x, 3 - z)),
    col_pairs(lambda x, z: (1 - x, z)),
)


def row_major(block):
    return with_layout_constraint(block, Layout(major_to_minor=tuple(range(block.ndim))))


def send(block, pairing):
    return row_major(lax.ppermute(row_major(block), pairing[0], pairing[1]))


def ring_bits(place):
    high = place // 2
    return (high ^ (place % 2), high)


def ring_place(low, high):
    return high * 2 + (low ^ high)


def gelu_parts(preact):
    value = preact.astype(jnp.float32)
    tangent = jnp.tanh(gelu_coeff * (value + cubic_coeff * value * value * value))
    activation = 0.5 * value * (1.0 + tangent)
    slope = 0.5 * (1.0 + tangent) + 0.5 * value * (1.0 - tangent * tangent) * gelu_coeff * (
        1.0 + 3.0 * cubic_coeff * value * value
    )
    return (activation, slope)


def contract_last(left, right):
    return lax.dot_general(
        left, right, (((1,), (1,)), ((), ())), preferred_element_type=jnp.float32
    )


def contract_first(left, right):
    return lax.dot_general(
        left, right, (((0,), (0,)), ((), ())), preferred_element_type=jnp.float32
    )


def thirds(block):
    width = block.shape[1] // 3
    return [block[:, part * width : (part + 1) * width] for part in range(3)]


def col_halves(block, crossed):
    both = jnp.stack([block, crossed])[None, None]
    rows = block.shape[0] // 2
    return [both[..., :rows, :], both[..., rows:, :]]


def col_gather_step(held, step):
    got = after_all([send(held[s], col_cube[(s + step) % 2]) for s in range(2)])
    return [jnp.concatenate([held[s], got[s]], axis=(s + step) % 2) for s in range(2)]


def add(left, right):
    return left.astype(jnp.float32) + right.astype(jnp.float32)


def cube_gather_step(held, cube, step):
    got = [send(held[s], cube[(s + step) % 3]) for s in range(3)]
    return [jnp.concatenate([held[s], got[s]], axis=(s + step) % 3) for s in range(3)]


def cube_scatter_step(own, got, cube, step):
    axes = [(s + step) % 3 for s in range(3)]
    total = [add(own[s], got[s]).astype(jnp.bfloat16) for s in range(3)]
    away = [lax.slice_in_dim(total[s], 1, 2, axis=axes[s]) for s in range(3)]
    own = [lax.slice_in_dim(total[s], 0, 1, axis=axes[s]) for s in range(3)]
    return own, [send(away[s], cube[axes[s]]) for s in range(3)]


def after_all(blocks, *earlier):
    return list(lax.optimization_barrier(tuple(blocks) + earlier)[: len(blocks)])


def after(block, *earlier):
    return lax.optimization_barrier((block,) + earlier)[0]


def by_core(core, own, other, axis):
    return jnp.where(
        core == 0,
        jnp.concatenate([own, other], axis=axis),
        jnp.concatenate([other, own], axis=axis),
    )


def body(inputs, cotangent, preact, up_weight, down_weight):
    row, col = lax.axis_index("row"), lax.axis_index("col")
    core, x_lo, y = row % 2, row // 2 % 2, row // 4
    x_hi, z = col // 4, col % 4
    y_bits, z_bits = ring_bits(y), ring_bits(z)
    half = preact.shape[1] // 2
    third = half // 3
    rows, features = inputs.shape
    token_count = rows * 8
    scale = 1.0 / math.sqrt(token_count)

    col_at_row, row_at_col = [], []
    for flips in range(8):
        a, b, c = flips // 4, flips // 2 % 2, flips % 2
        block = ring_place(y_bits[0] ^ a, y_bits[1] ^ b) * 2 + (x_lo ^ c)
        bits = ring_bits(block % 4)
        col_at_row.append((bits[0] ^ z_bits[0]) * 4 + (bits[1] ^ z_bits[1]) * 2 + (block // 4 ^ x_hi))
        block = (x_hi ^ c) * 4 + ring_place(z_bits[0] ^ a, z_bits[1] ^ b)
        bits = ring_bits(block // 2)
        row_at_col.append((bits[0] ^ y_bits[0]) * 4 + (bits[1] ^ y_bits[1]) * 2 + (block % 2 ^ x_lo))

    def halves_of(block, axis):
        mine = lax.dynamic_slice_in_dim(block, core * half, half, axis)
        other = lax.dynamic_slice_in_dim(block, (1 - core) * half, half, axis)
        return mine, other

    def as_parts(block):
        return [part[None, None, None] for part in thirds(block)]

    def in_row_order(blocks, places):
        count = blocks.shape[1]
        picked = [lax.dynamic_index_in_dim(blocks, at, 0, keepdims=False) for at in places]
        ordered = jnp.stack(picked)
        return jnp.concatenate([ordered, send(ordered, core_swap)], axis=2).reshape(2, 2, 2, count, -1)

    mine, other = halves_of(preact, 1)
    other = send(other, core_swap)
    crossed = send(cotangent, col_cube[2])
    saved = as_parts(by_core(core, mine, other, 0))
    merged = after_all([crossed] + saved)
    crossed, saved = merged[0], merged[1:]
    saved = cube_gather_step(saved, row_cube, 0)
    cots = col_halves(cotangent, crossed)
    cots = col_gather_step(cots, 0)
    acts, slopes = [], []
    for part in saved:
        activation, slope = gelu_parts(part)
        acts.append(activation.astype(jnp.bfloat16))
        slopes.append(slope)
    mine, other = halves_of(down_weight, 0)
    down_half = jnp.concatenate([mine, send(other, core_swap)], axis=1)
    merged = after_all(cots + acts, down_half)
    cots, acts = merged[:2], merged[2:]
    cots = col_gather_step(cots, 1)
    acts = cube_gather_step(acts, row_cube, 1)
    cots = after_all(cots, *acts)
    whole = jnp.concatenate(cots, axis=3).reshape(8, rows, features)
    all_cot = in_row_order(whole, col_at_row)

    def hidden_product(s, at):
        tokens = lax.slice_in_dim(all_cot, at, at + 1, axis=(s + 2) % 3)
        weight = down_half[s * third : (s + 1) * third]
        product = contract_last(tokens.reshape(4 * rows, -1), weight).astype(jnp.bfloat16)
        return row_major(product.reshape(tokens.shape[:4] + (third,)))

    away = [hidden_product(s, 1) for s in range(3)]
    got = [send(away[s], row_cube[(s + 2) % 3]) for s in range(3)]
    own = [hidden_product(s, 0) for s in range(3)]

    own, got = cube_scatter_step(own, got, row_cube, 1)
    crossed = send(after(inputs, *own), col_cube[2])
    got = after_all(got, crossed)
    total = [add(own[s], got[s]).astype(jnp.bfloat16) for s in range(3)]
    got = [send(total[s], row_cube[s]) for s in range(3)]
    pres = []
    for s in range(3):
        near_got, far_got = [lax.slice_in_dim(got[s], at, at + 1, axis=s) for at in (0, 1)]
        hidden = add(total[s], jnp.concatenate([far_got, near_got], axis=s))
        pres.append(row_major((hidden * slopes[s]).astype(jnp.bfloat16)))
    near = col_gather_step(after_all(col_halves(inputs, crossed), *pres), 0)
    pres = cube_gather_step(pres, row_cube, 1)
    pres = after_all(pres, *near)

    last = [send(pres[s], row_cube[(s + 2) % 3]) for s in range(3)]

    near = col_gather_step(after_all(near, *pres), 1)
    mine, other = halves_of(after(up_weight, *pres), 1)
    up_half = jnp.concatenate([mine, send(other, core_swap)], axis=0)
    given = []
    for h in range(2):
        block = near[h].reshape(8, rows // 2, features)
        given.append(in_row_order(block, col_at_row).reshape(token_count // 2, -1))
    last = after_all(last, up_half, *given)

    halves = [slice(h * rows // 2, (h + 1) * rows // 2) for h in range(2)]
    moving = after_all(acts, *last)
    moving = [[act[..., part, :] for act in moving] for part in halves]
    got_acts = [[send(moving[0][s], row_cube[(s + 2) % 3]) for s in range(3)]]
    own, away, got, all_pre = [], [], [], []
    for h, part in enumerate(halves):
        pre = [
            jnp.concatenate([pres[s][..., part, :], last[s][..., part, :]], axis=(s + 2) % 3) for s in range(3)
        ]
        pre = jnp.concatenate([block.reshape(token_count // 2, third) for block in pre], axis=1)
        all_pre.append(pre)
        partial = contract_last(pre, up_half).astype(jnp.bfloat16)
        swapped = send(partial[:, features:], core_swap)
        blocks = add(partial[:, :features], swapped).astype(jnp.bfloat16).reshape(8, rows // 2, features)
        picked = [lax.dynamic_index_in_dim(blocks, at, 0, keepdims=False) for at in row_at_col]
        picked = jnp.stack(picked).reshape(2, 2, 2, rows // 2, features)
        own.append(lax.slice_in_dim(picked, 0, 1, axis=h))
        away.append(lax.slice_in_dim(picked, 1, 2, axis=h))
        if h:
            merged = after_all([away[h]] + moving[1] + got_acts[0])
            away[h], moving[1], got_acts[0] = merged[0], merged[1:4], merged[4:]
            got_acts.append([send(moving[1][s], row_cube[(s + 2) % 3]) for s in range(3)])
        got.append(send(away[h], col_cube[h]))

    up = sum(contract_first(after(given[h], *away), all_pre[h]) for h in range(2))
    up = (up * scale).astype(jnp.bfloat16)

    def down_product(s, at, act, *earlier):
        tokens, act = after_all([all_cot, act], *earlier)
        tokens = lax.slice_in_dim(tokens, at, at + 1, axis=(s + 2) % 3).reshape(4 * rows, -1)
        return contract_first(act.reshape(4 * rows, third), tokens)

    down = [down_product(s, 0, acts[s], *away) for s in range(3)]
    merged = after_all(got + [up] + down)
    got, up, down = merged[:2], merged[2], merged[3:]
    total = [add(own[s], got[s]).astype(jnp.bfloat16) for s in range(2)]
    own = [lax.slice_in_dim(total[s], 0, 1, axis=1 - s) for s in range(2)]
    away = [lax.slice_in_dim(total[s], 1, 2, axis=1 - s) for s in range(2)]
    got = [send(away[s], col_cube[1 - s]) for s in range(2)]
    merged = after_all(got + got_acts[1])
    got, got_acts[1] = merged[:2], merged[2:]
    total = [add(own[s], got[s]).astype(jnp.bfloat16)[0, 0] for s in range(2)]
    total = jnp.concatenate(total, axis=1)
    got = send(total[1], col_cube[2])

    for s in range(3):
        act = jnp.concatenate([got_acts[0][s], got_acts[1][s]], axis=3)
        down[s] = ((down[s] + down_product(s, 1, act, total)) * scale).astype(jnp.bfloat16)
    merged = after_all([got] + down)
    got, down = merged[0], merged[1:]
    up = after(up, total)
    up_grad = by_core(core, up[:features], send(up[features:], core_swap), 1)
    down = jnp.concatenate(down, axis=0)
    down_grad = by_core(core, down[:, :features], send(down[:, features:], core_swap), 0)
    got, up_grad, down_grad = after_all([got, up_grad, down_grad])
    input_grad = add(total[0], got).astype(jnp.bfloat16)
    return (input_grad, up_grad, down_grad)


def solution(mesh):
    return jax.shard_map(
        body,
        mesh=mesh,
        in_specs=(
            P("col", "row"),
            P("col", "row"),
            P("row", "col"),
            P("row", "col"),
            P("col", "row"),
        ),
        out_specs=(P("col", "row"), P("row", "col"), P("col", "row")),
        check_vma=False,
    )
```

```python
import math

import jax
import jax.numpy as jnp
from jax import lax
from jax.experimental.layout import Layout, with_layout_constraint
from jax.sharding import PartitionSpec as P

gelu_coeff = 0.7978845608
cubic_coeff = 0.044715


def row_pairs(flip):
    pairs = []
    for y in range(4):
        for x in range(2):
            for core in range(2):
                to_y, to_x, to_core = flip(y, x, core)
                pairs.append(((y * 2 + x) * 2 + core, (to_y * 2 + to_x) * 2 + to_core))
    return ("row", pairs)


def col_pairs(flip):
    pairs = []
    for x in range(2):
        for z in range(4):
            to_x, to_z = flip(x, z)
            pairs.append((x * 4 + z, to_x * 4 + to_z))
    return ("col", pairs)


core_swap = row_pairs(lambda y, x, core: (y, x, 1 - core))
row_cube = (
    row_pairs(lambda y, x, core: (y ^ 1, x, core)),
    row_pairs(lambda y, x, core: (3 - y, x, core)),
    row_pairs(lambda y, x, core: (y, 1 - x, core)),
)
col_cube = (
    col_pairs(lambda x, z: (x, z ^ 1)),
    col_pairs(lambda x, z: (x, 3 - z)),
    col_pairs(lambda x, z: (1 - x, z)),
)


def row_major(block):
    return with_layout_constraint(block, Layout(major_to_minor=tuple(range(block.ndim))))


def send(block, pairing):
    return row_major(lax.ppermute(row_major(block), pairing[0], pairing[1]))


def ring_bits(place):
    high = place // 2
    return (high ^ (place % 2), high)


def ring_place(low, high):
    return high * 2 + (low ^ high)


def gelu_parts(preact):
    value = preact.astype(jnp.float32)
    tangent = jnp.tanh(gelu_coeff * (value + cubic_coeff * value * value * value))
    activation = 0.5 * value * (1.0 + tangent)
    slope = 0.5 * (1.0 + tangent) + 0.5 * value * (1.0 - tangent * tangent) * gelu_coeff * (
        1.0 + 3.0 * cubic_coeff * value * value
    )
    return (activation, slope)


def contract_last(left, right):
    return lax.dot_general(
        left, right, (((1,), (1,)), ((), ())), preferred_element_type=jnp.float32
    )


def contract_first(left, right):
    return lax.dot_general(
        left, right, (((0,), (0,)), ((), ())), preferred_element_type=jnp.float32
    )


def thirds(block):
    width = block.shape[1] // 3
    return [block[:, part * width : (part + 1) * width] for part in range(3)]


def col_halves(block, crossed):
    both = jnp.stack([block, crossed])[None, None]
    rows = block.shape[0] // 2
    return [both[..., :rows, :], both[..., rows:, :]]


def col_gather_step(held, step):
    got = after_all([send(held[s], col_cube[(s + step) % 2]) for s in range(2)])
    return [jnp.concatenate([held[s], got[s]], axis=(s + step) % 2) for s in range(2)]


def add(left, right):
    return left.astype(jnp.float32) + right.astype(jnp.float32)


def cube_gather_step(held, cube, step):
    got = [send(held[s], cube[(s + step) % 3]) for s in range(3)]
    return [jnp.concatenate([held[s], got[s]], axis=(s + step) % 3) for s in range(3)]


def cube_scatter_step(own, got, cube, step):
    axes = [(s + step) % 3 for s in range(3)]
    total = [add(own[s], got[s]).astype(jnp.bfloat16) for s in range(3)]
    away = [lax.slice_in_dim(total[s], 1, 2, axis=axes[s]) for s in range(3)]
    own = [lax.slice_in_dim(total[s], 0, 1, axis=axes[s]) for s in range(3)]
    return own, [send(away[s], cube[axes[s]]) for s in range(3)]


def after_all(blocks, *earlier):
    return list(lax.optimization_barrier(tuple(blocks) + earlier)[: len(blocks)])


def after(block, *earlier):
    return lax.optimization_barrier((block,) + earlier)[0]


def by_core(core, own, other, axis):
    return jnp.where(
        core == 0,
        jnp.concatenate([own, other], axis=axis),
        jnp.concatenate([other, own], axis=axis),
    )


def body(inputs, cotangent, preact, up_weight, down_weight):
    row, col = lax.axis_index("row"), lax.axis_index("col")
    core, x_lo, y = row % 2, row // 2 % 2, row // 4
    x_hi, z = col // 4, col % 4
    y_bits, z_bits = ring_bits(y), ring_bits(z)
    half = preact.shape[1] // 2
    third = half // 3
    rows, features = inputs.shape
    token_count = rows * 8
    scale = 1.0 / math.sqrt(token_count)

    col_at_row, row_at_col = [], []
    for flips in range(8):
        a, b, c = flips // 4, flips // 2 % 2, flips % 2
        block = ring_place(y_bits[0] ^ a, y_bits[1] ^ b) * 2 + (x_lo ^ c)
        bits = ring_bits(block % 4)
        col_at_row.append((bits[0] ^ z_bits[0]) * 4 + (bits[1] ^ z_bits[1]) * 2 + (block // 4 ^ x_hi))
        block = (x_hi ^ c) * 4 + ring_place(z_bits[0] ^ a, z_bits[1] ^ b)
        bits = ring_bits(block // 2)
        row_at_col.append((bits[0] ^ y_bits[0]) * 4 + (bits[1] ^ y_bits[1]) * 2 + (block % 2 ^ x_lo))

    def halves_of(block, axis):
        mine = lax.dynamic_slice_in_dim(block, core * half, half, axis)
        other = lax.dynamic_slice_in_dim(block, (1 - core) * half, half, axis)
        return mine, other

    def as_parts(block):
        return [part[None, None, None] for part in thirds(block)]

    def in_row_order(blocks, places):
        count = blocks.shape[1]
        picked = [lax.dynamic_index_in_dim(blocks, at, 0, keepdims=False) for at in places]
        ordered = jnp.stack(picked)
        return jnp.concatenate([ordered, send(ordered, core_swap)], axis=2).reshape(2, 2, 2, count, -1)

    mine, other = halves_of(preact, 1)
    other = send(other, core_swap)
    crossed = send(cotangent, col_cube[2])
    saved = as_parts(by_core(core, mine, other, 0))
    merged = after_all([crossed] + saved)
    crossed, saved = merged[0], merged[1:]
    saved = cube_gather_step(saved, row_cube, 0)
    cots = col_halves(cotangent, crossed)
    cots = col_gather_step(cots, 0)
    acts, slopes = [], []
    for part in saved:
        activation, slope = gelu_parts(part)
        acts.append(activation.astype(jnp.bfloat16))
        slopes.append(slope)
    mine, other = halves_of(down_weight, 0)
    down_half = jnp.concatenate([mine, send(other, core_swap)], axis=1)
    merged = after_all(cots + acts, down_half)
    cots, acts = merged[:2], merged[2:]
    cots = col_gather_step(cots, 1)
    acts = cube_gather_step(acts, row_cube, 1)
    cots = after_all(cots, *acts)
    whole = jnp.concatenate(cots, axis=3).reshape(8, rows, features)
    all_cot = in_row_order(whole, col_at_row)

    def hidden_product(s, at):
        tokens = lax.slice_in_dim(all_cot, at, at + 1, axis=(s + 2) % 3)
        weight = down_half[s * third : (s + 1) * third]
        product = contract_last(tokens.reshape(4 * rows, -1), weight).astype(jnp.bfloat16)
        return row_major(product.reshape(tokens.shape[:4] + (third,)))

    away = [hidden_product(s, 1) for s in range(3)]
    got = [send(away[s], row_cube[(s + 2) % 3]) for s in range(3)]
    own = [hidden_product(s, 0) for s in range(3)]

    crossed = send(inputs, col_cube[2])
    near = col_gather_step(col_halves(inputs, after(crossed, *away)), 0)
    got = after_all(got, *near)
    own, got = cube_scatter_step(own, got, row_cube, 1)
    total = [add(own[s], got[s]).astype(jnp.bfloat16) for s in range(3)]
    got = [send(total[s], row_cube[s]) for s in range(3)]
    near = col_gather_step(after_all(near, *total), 1)
    got = after_all(got, *near)
    pres = []
    for s in range(3):
        near_got, far_got = [lax.slice_in_dim(got[s], at, at + 1, axis=s) for at in (0, 1)]
        hidden = add(total[s], jnp.concatenate([far_got, near_got], axis=s))
        pres.append(row_major((hidden * slopes[s]).astype(jnp.bfloat16)))
    pres = cube_gather_step(pres, row_cube, 1)

    last = [send(pres[s], row_cube[(s + 2) % 3]) for s in range(3)]

    near = after_all(near, *pres)
    mine, other = halves_of(after(up_weight, *pres), 1)
    up_half = jnp.concatenate([mine, send(other, core_swap)], axis=0)
    given = []
    for h in range(2):
        block = near[h].reshape(8, rows // 2, features)
        given.append(in_row_order(block, col_at_row).reshape(token_count // 2, -1))
    last = after_all(last, up_half, *given)

    halves = [slice(h * rows // 2, (h + 1) * rows // 2) for h in range(2)]
    moving = after_all(acts, *last)
    moving = [[act[..., part, :] for act in moving] for part in halves]
    got_acts = [[send(moving[0][s], row_cube[(s + 2) % 3]) for s in range(3)]]
    own, away, got, all_pre = [], [], [], []
    for h, part in enumerate(halves):
        pre = [
            jnp.concatenate([pres[s][..., part, :], last[s][..., part, :]], axis=(s + 2) % 3) for s in range(3)
        ]
        pre = jnp.concatenate([block.reshape(token_count // 2, third) for block in pre], axis=1)
        all_pre.append(pre)
        partial = contract_last(pre, up_half).astype(jnp.bfloat16)
        swapped = send(partial[:, features:], core_swap)
        blocks = add(partial[:, :features], swapped).astype(jnp.bfloat16).reshape(8, rows // 2, features)
        picked = [lax.dynamic_index_in_dim(blocks, at, 0, keepdims=False) for at in row_at_col]
        picked = jnp.stack(picked).reshape(2, 2, 2, rows // 2, features)
        own.append(lax.slice_in_dim(picked, 0, 1, axis=h))
        away.append(lax.slice_in_dim(picked, 1, 2, axis=h))
        if h:
            merged = after_all([away[h]] + moving[1] + got_acts[0])
            away[h], moving[1], got_acts[0] = merged[0], merged[1:4], merged[4:]
            got_acts.append([send(moving[1][s], row_cube[(s + 2) % 3]) for s in range(3)])
        got.append(send(away[h], col_cube[h]))

    up = sum(contract_first(after(given[h], *away), all_pre[h]) for h in range(2))
    up = (up * scale).astype(jnp.bfloat16)

    def down_product(s, at, act, *earlier):
        tokens, act = after_all([all_cot, act], *earlier)
        tokens = lax.slice_in_dim(tokens, at, at + 1, axis=(s + 2) % 3).reshape(4 * rows, -1)
        return contract_first(act.reshape(4 * rows, third), tokens)

    down = [down_product(s, 0, acts[s], *away) for s in range(3)]
    merged = after_all(got + [up] + down)
    got, up, down = merged[:2], merged[2], merged[3:]
    total = [add(own[s], got[s]).astype(jnp.bfloat16) for s in range(2)]
    own = [lax.slice_in_dim(total[s], 0, 1, axis=1 - s) for s in range(2)]
    away = [lax.slice_in_dim(total[s], 1, 2, axis=1 - s) for s in range(2)]
    got = [send(away[s], col_cube[1 - s]) for s in range(2)]
    merged = after_all(got + got_acts[1])
    got, got_acts[1] = merged[:2], merged[2:]
    total = [add(own[s], got[s]).astype(jnp.bfloat16)[0, 0] for s in range(2)]
    total = jnp.concatenate(total, axis=1)
    got = send(total[1], col_cube[2])

    for s in range(3):
        act = jnp.concatenate([got_acts[0][s], got_acts[1][s]], axis=3)
        down[s] = ((down[s] + down_product(s, 1, act, total)) * scale).astype(jnp.bfloat16)
    merged = after_all([got] + down)
    got, down = merged[0], merged[1:]
    up = after(up, total)
    up_grad = by_core(core, up[:features], send(up[features:], core_swap), 1)
    down = jnp.concatenate(down, axis=0)
    down_grad = by_core(core, down[:, :features], send(down[:, features:], core_swap), 0)
    got, up_grad, down_grad = after_all([got, up_grad, down_grad])
    input_grad = add(total[0], got).astype(jnp.bfloat16)
    return (input_grad, up_grad, down_grad)


def solution(mesh):
    return jax.shard_map(
        body,
        mesh=mesh,
        in_specs=(
            P("col", "row"),
            P("col", "row"),
            P("row", "col"),
            P("row", "col"),
            P("col", "row"),
        ),
        out_specs=(P("col", "row"), P("row", "col"), P("col", "row")),
        check_vma=False,
    )
```
